32 devices in a mesh: dp: 2 (over y), seq: 4 (over z), section: 4 (over x, core).
Axes of the slice: x: 2, y: 2, z: 4, core: 2. Of those that a mesh axis runs over, the one named last changes fastest.
Arguments:
- signal: bfloat16 [2, 2560, 1280], P('dp', 'seq'), may hold values from -6 to 6
- kernel: bfloat16 [1536, 5, 1280], P('section'), may hold values from -0.078125 to 0.078125
- trunk_grad: bfloat16 [2, 1280, 1536], P('dp', ('seq', 'section')), may hold values from -6 to 6
Outputs:
- weight_grad: float32 [1536, 5, 1280], P(('section', 'seq'))
- input_grad: bfloat16 [2, 1280, 2560], P('dp', 'section', 'seq')
The draws below stay inside these ranges and needn't reach their ends.
All inputs are finite; a program needn't handle non-finite values.
Results may differ from the reference program's by a relative error of at most 0.019.
Values may be sent and summed in bfloat16 or wider, within the bound.
A program may use at most 64 MiB of HBM per device.

```python
import jax
import jax.numpy as jnp
from jax import lax

C_IN = 1280
C_OUT = 1536
K = 5
L_DEV = 640
L = 2560
LOUT = 1280
CO_DEV = 384
N_DP = 2
N_SEQ = 4
N_SECTION = 4


def strengthened(entries, rng, source, target, shards_of, factor):
    owner, partner = [(jnp.arange(entries.shape[position]) // (entries.shape[position] // shards_of)).reshape([-1 if axis == position else 1 for axis in range(entries.ndim)]) for position in (source, target)]
    chosen = jax.random.permutation(rng, shards_of)[partner]
    strong = (owner == chosen) | (owner == (partner + shards_of // 2) % shards_of)
    return jnp.where(strong, factor * entries, entries)


def block_scale(own_key, extent, shards, least, high):
    loudness = 1.0
    for axis_at, blocks in shards:
        heights = jax.random.uniform(jax.random.fold_in(jax.random.fold_in(own_key, 6), axis_at), (blocks,), jnp.float32, least / len(shards), high / len(shards))
        loudness = loudness * jnp.repeat(jnp.exp(heights), extent[axis_at] // blocks).reshape((-1,) + (1,) * (len(extent) - 1 - axis_at))
    return loudness


def scatter_about(key, shape, spread, bound, split=(), held_as=jnp.bfloat16):
    drawn = jax.random.normal(key, shape, jnp.float32) * spread
    if len(split) > 0:
        drawn = block_scale(key, shape, split, -0.22, 0.18) * drawn
    return jnp.clip(drawn, min=-bound, max=bound).astype(held_as)


def gaussian_with(stream_key, shape, scale, reach, cuts, heavy, dtype=jnp.bfloat16):
    array = scale * jax.random.normal(stream_key, shape, jnp.float32)
    if cuts:
        array = array * block_scale(stream_key, shape, cuts, -0.22, 0.18)
    return jnp.clip(strengthened(array, jax.random.fold_in(stream_key, 3), *heavy), -reach, reach).astype(dtype)


def setup_inputs(seed: int = 0) -> dict:
    key_list = jax.random.split(jax.random.key(seed), 4)
    signal = scatter_about(key_list[0], (N_DP, L, C_IN), 1.0, 6.0, ((0, 2), (1, 4)))
    kernel = scatter_about(key_list[1], (C_OUT, K, C_IN), (K * C_IN) ** -0.5, 0.078125, ((0, 4),))
    trunk_grad = gaussian_with(key_list[2], (N_DP, LOUT, C_OUT), 1.0, 6.0, ((0, 2), (1, 16)), (1, 2, 16, 2.0))
    return dict(signal=signal, kernel=kernel, trunk_grad=trunk_grad)


def gelu_slope(values):
    normal_cdf = 0.5 * (1.0 + jax.scipy.special.erf(values * 0.7071067811865476))
    density = jnp.exp(-0.5 * values * values) * 0.3989422804014327
    return normal_cdf + values * density


def rounded(values):
    return lax.optimization_barrier(values.astype(jnp.bfloat16)).astype(jnp.float32)


def reference(signal, kernel, trunk_grad):
    weight_sum = jnp.zeros((C_OUT, K, C_IN), jnp.float32)
    input_grads = []
    for replica in range(N_DP):
        padded = jnp.pad(signal[replica], ((2, 2), (0, 0)))
        linear = jnp.zeros((L, C_OUT), jnp.float32)
        for offset in range(K):
            linear = linear + jnp.dot(padded[offset:offset + L], kernel[:, offset, :].T, preferred_element_type=jnp.float32)
        grad_hidden = 0.5 * jnp.repeat(trunk_grad[replica].astype(jnp.float32), 2, axis=0)
        grad_pre = (grad_hidden * gelu_slope(linear)).astype(jnp.bfloat16)
        for block in range(N_SEQ):
            begin = block * L_DEV
            grad_block = grad_pre[begin:begin + L_DEV]
            taps = []
            for offset in range(K):
                window = padded[begin + offset:begin + offset + L_DEV]
                taps.append(jnp.dot(grad_block.T, window, preferred_element_type=jnp.float32))
            weight_sum = weight_sum + rounded(jnp.stack(taps, axis=1))
        grad_padded = jnp.pad(grad_pre, ((2, 2), (0, 0)))
        input_sum = jnp.zeros((L, C_IN), jnp.float32)
        for group in range(N_SECTION):
            first_col = group * CO_DEV
            term = jnp.zeros((L, C_IN), jnp.float32)
            for offset in range(K):
                grad_slice = grad_padded[4 - offset:4 - offset + L, first_col:first_col + CO_DEV]
                kernel_slice = kernel[first_col:first_col + CO_DEV, offset, :]
                term = term + jnp.dot(grad_slice, kernel_slice, preferred_element_type=jnp.float32)
            input_sum = input_sum + rounded(term)
        input_grads.append(input_sum.T.astype(jnp.bfloat16))
    return weight_sum, jnp.stack(input_grads)
```

```python
import jax
import jax.numpy as jnp
from jax import lax
from jax.sharding import PartitionSpec as P


def edges(block, axis, width):
    count = lax.axis_size(axis)
    forward = [(i, i + 1) for i in range(count - 1)]
    backward = [(target, source) for source, target in forward]
    low = lax.ppermute(block[-width:], axis, forward)
    high = lax.ppermute(block[:width], axis, backward)
    return jnp.concatenate([low, block, high], axis=0)


def gelu_slope(values):
    normal_cdf = 0.5 * (1.0 + jax.scipy.special.erf(values * 0.7071067811865476))
    density = jnp.exp(-0.5 * values * values) * 0.3989422804014327
    return normal_cdf + values * density


def shards(signal, kernel, trunk_grad):
    n_dp = lax.axis_size("dp")
    n_section = lax.axis_size("section")
    me = lax.axis_index("dp")
    local = signal[0]
    length, c_in = local.shape
    c_out, taps_count, _ = kernel.shape
    width = taps_count // 2
    share = c_in // n_dp
    flat = jnp.transpose(kernel, (1, 0, 2)).reshape(taps_count * c_out, c_in)

    rows = trunk_grad.shape[1]
    trunk = jnp.transpose(trunk_grad[0].reshape(rows, n_section, c_out), (1, 0, 2))
    pooled = lax.all_to_all(trunk, "section", split_axis=0, concat_axis=0).reshape(
        n_section * rows, c_out
    )
    padded = edges(local, "seq", width)

    rings = [[(i, (i + step) % n_dp) for i in range(n_dp)] for step in range(n_dp)]

    def columns(owner):
        return lax.dynamic_slice_in_dim(padded, owner * share, share, axis=1)

    windows = [columns(me)]
    for step in range(1, n_dp):
        windows.append(lax.ppermute(columns((me + step) % n_dp), "dp", rings[step]))

    product = lax.dot_general(
        padded, flat, (((1,), (1,)), ((), ())), preferred_element_type=jnp.float32
    )
    linear = product[0:length, 0:c_out]
    for tap in range(1, taps_count):
        linear = linear + product[tap : tap + length, tap * c_out : (tap + 1) * c_out]
    grad_hidden = 0.5 * jnp.repeat(pooled.astype(jnp.float32), 2, axis=0)
    grad_pre = (grad_hidden * gelu_slope(linear)).astype(jnp.bfloat16)

    grads = [grad_pre]
    for step in range(1, n_dp):
        grads.append(lax.ppermute(grad_pre, "dp", rings[step]))
    grad_ext = edges(grad_pre, "seq", width)

    all_grads = jnp.concatenate(grads, axis=0)
    taps = []
    for tap in range(taps_count):
        window = jnp.concatenate([w[tap : tap + length] for w in windows], axis=0)
        taps.append(
            lax.dot_general(
                all_grads, window, (((0,), (0,)), ((), ())), preferred_element_type=jnp.float32
            ).astype(jnp.bfloat16)
        )
    partial = jnp.stack(taps, axis=1)
    weight_rows = lax.psum_scatter(partial, "seq", scatter_dimension=0, tiled=True)

    stacked = jnp.concatenate(
        [grad_ext[2 * width - tap : 2 * width - tap + length] for tap in range(taps_count)], axis=1
    )
    summed = lax.dot_general(
        flat, stacked, (((0,), (1,)), ((), ())), preferred_element_type=jnp.float32
    ).astype(jnp.bfloat16)
    input_rows = lax.psum_scatter(summed, "section", scatter_dimension=0, tiled=True)

    weight_grad = jnp.zeros(weight_rows.shape[:2] + (c_in,), jnp.float32)
    weight_grad = lax.dynamic_update_slice_in_dim(
        weight_grad, weight_rows.astype(jnp.float32), me * share, axis=2
    )
    for step in range(1, n_dp):
        other = lax.ppermute(weight_rows, "dp", rings[step])
        weight_grad = lax.dynamic_update_slice_in_dim(
            weight_grad, other.astype(jnp.float32), ((me - step) % n_dp) * share, axis=2
        )
    return (weight_grad, input_rows[None])


def solution(mesh):
    return jax.shard_map(
        shards,
        mesh=mesh,
        in_specs=(
            P("dp", "seq", None),
            P("section", None, None),
            P("dp", ("seq", "section"), None),
        ),
        out_specs=(P(("section", "seq"), None, None), P("dp", "section", "seq")),
        check_vma=False,
    )
```

```python
import functools

import jax
import jax.numpy as jnp
from jax import lax
from jax.experimental import pallas as pl
from jax.experimental.pallas import tpu as pltpu
from jax.sharding import PartitionSpec as P


def edges(block, axis, width):
    count = lax.axis_size(axis)
    forward = [(i, i + 1) for i in range(count - 1)]
    backward = [(target, source) for source, target in forward]
    low = lax.ppermute(block[-width:], axis, forward)
    high = lax.ppermute(block[:width], axis, backward)
    return jnp.concatenate([low, block, high], axis=0)


def gelu_slope(values):
    normal_cdf = 0.5 * (1.0 + jax.scipy.special.erf(values * 0.7071067811865476))
    density = jnp.exp(-0.5 * values * values) * 0.3989422804014327
    return normal_cdf + values * density


def shards(signal, kernel, trunk_grad):
    n_dp = lax.axis_size("dp")
    n_section = lax.axis_size("section")
    me = lax.axis_index("dp")
    local = signal[0]
    length, c_in = local.shape
    c_out, taps_count, _ = kernel.shape
    width = taps_count // 2
    share = c_in // n_dp
    flat = jnp.transpose(kernel, (1, 0, 2)).reshape(taps_count * c_out, c_in)

    rows = trunk_grad.shape[1]
    trunk = jnp.transpose(trunk_grad[0].reshape(rows, n_section, c_out), (1, 0, 2))
    pooled = lax.all_to_all(trunk, "section", split_axis=0, concat_axis=0).reshape(
        n_section * rows, c_out
    )
    padded = edges(local, "seq", width)

    rings = [[(i, (i + step) % n_dp) for i in range(n_dp)] for step in range(n_dp)]

    def columns(owner):
        return lax.dynamic_slice_in_dim(padded, owner * share, share, axis=1)

    windows = [columns(me)]
    for step in range(1, n_dp):
        windows.append(lax.ppermute(columns((me + step) % n_dp), "dp", rings[step]))

    product = lax.dot_general(
        padded, flat, (((1,), (1,)), ((), ())), preferred_element_type=jnp.float32
    )
    linear = product[0:length, 0:c_out]
    for tap in range(1, taps_count):
        linear = linear + product[tap : tap + length, tap * c_out : (tap + 1) * c_out]
    grad_hidden = 0.5 * jnp.repeat(pooled.astype(jnp.float32), 2, axis=0)
    grad_pre = (grad_hidden * gelu_slope(linear)).astype(jnp.bfloat16)

    grads = [grad_pre]
    for step in range(1, n_dp):
        grads.append(lax.ppermute(grad_pre, "dp", rings[step]))
    grad_ext = edges(grad_pre, "seq", width)

    all_grads = jnp.concatenate(grads, axis=0)
    taps = []
    for tap in range(taps_count):
        window = jnp.concatenate([w[tap : tap + length] for w in windows], axis=0)
        taps.append(
            lax.dot_general(
                all_grads, window, (((0,), (0,)), ((), ())), preferred_element_type=jnp.float32
            ).astype(jnp.bfloat16)
        )
    partial = jnp.stack(taps, axis=1)
    weight_rows = lax.psum_scatter(partial, "seq", scatter_dimension=0, tiled=True)

    stacked = jnp.concatenate(
        [grad_ext[2 * width - tap : 2 * width - tap + length] for tap in range(taps_count)], axis=1
    )
    summed = lax.dot_general(
        flat, stacked, (((0,), (1,)), ((), ())), preferred_element_type=jnp.float32
    ).astype(jnp.bfloat16)
    input_rows = lax.psum_scatter(summed, "section", scatter_dimension=0, tiled=True)

    weight_grad = jnp.zeros(weight_rows.shape[:2] + (c_in,), jnp.float32)
    weight_grad = lax.dynamic_update_slice_in_dim(
        weight_grad, weight_rows.astype(jnp.float32), me * share, axis=2
    )
    for step in range(1, n_dp):
        other = lax.ppermute(weight_rows, "dp", rings[step])
        weight_grad = lax.dynamic_update_slice_in_dim(
            weight_grad, other.astype(jnp.float32), ((me - step) % n_dp) * share, axis=2
        )
    return (weight_grad, input_rows[None])


MESH = pl.DeviceIdType.MESH
EDGE = 16


def fused_kernel(
    n_seq,
    n_section,
    signal,
    flat_hbm,
    trunk,
    weight_out,
    input_out,
    ext,
    flat,
    pooled,
    prod,
    linear,
    grad_b,
    grad_f,
    grad_halo,
    stacked,
    grad_t,
    other,
    shift,
    windows,
    input_part,
    input_recv,
    weight_f,
    ring_send,
    ring_up,
    ring_down,
    last_send,
    last_recv,
    load_sem,
    halo_sem,
    trunk_sem,
    signal_sem,
    grad_sem,
    input_sem,
    ring_send_sem,
    ring_up_sem,
    ring_down_sem,
    last_sem,
):
    f32, bf16 = jnp.float32, jnp.bfloat16
    d, z, s = lax.axis_index("dp"), lax.axis_index("seq"), lax.axis_index("section")
    length, c_in = signal.shape
    c_out = pooled.shape[1]
    rows = trunk.shape[0]
    taps = flat.shape[0] // c_out
    half = c_in // 2
    part = length // 2
    width = taps // 2
    share = c_out // n_seq
    block = c_in // n_section
    end = EDGE + length
    core = lax.rem(s, 2)
    sibling = s + 1 - 2 * core
    last = n_seq - 1

    def to_dp():
        return {"dp": 1 - d}

    def to_seq(target):
        return {"seq": target}

    def to_section(target):
        return {"section": target}

    def remote(src, dst, send, recv, target):
        return pltpu.make_async_remote_copy(
            src_ref=src,
            dst_ref=dst,
            send_sem=send,
            recv_sem=recv,
            device_id=target,
            device_id_type=MESH,
        )

    mine = pl.ds(pl.multiple_of(d * half, 128), half)
    theirs = pl.ds(pl.multiple_of((1 - d) * half, 128), half)
    own_rows = pl.ds(pl.multiple_of(s * rows, EDGE), rows)

    load_signal = pltpu.make_async_copy(signal, ext.at[EDGE:end], load_sem.at[0])
    load_flat = pltpu.make_async_copy(flat_hbm, flat, load_sem.at[1])
    load_trunk = pltpu.make_async_copy(
        trunk.at[:, pl.ds(pl.multiple_of(s * c_out, 128), c_out)], pooled.at[own_rows], load_sem.at[2]
    )
    load_signal.start()
    load_flat.start()
    load_trunk.start()

    @pl.when(z == 0)
    def _():
        ext[0:EDGE] = jnp.zeros((EDGE, c_in), bf16)
        grad_halo[0] = jnp.zeros((EDGE, c_out), bf16)

    @pl.when(z == last)
    def _():
        ext[end : end + EDGE] = jnp.zeros((EDGE, c_in), bf16)
        grad_halo[1] = jnp.zeros((EDGE, c_out), bf16)

    barrier = pltpu.get_barrier_semaphore()
    pl.semaphore_signal(barrier, inc=1, device_id=to_dp(), device_id_type=MESH)
    for step in range(1, n_section):
        pl.semaphore_signal(
            barrier, inc=1, device_id=to_section(lax.rem(s + step, n_section)), device_id_type=MESH
        )

    @pl.when(z > 0)
    def _():
        pl.semaphore_signal(barrier, inc=1, device_id=to_seq(z - 1), device_id_type=MESH)

    @pl.when(z < last)
    def _():
        pl.semaphore_signal(barrier, inc=1, device_id=to_seq(z + 1), device_id_type=MESH)

    @pl.when(jnp.logical_and(z > 0, z < last))
    def _():
        pl.semaphore_wait(barrier, n_section + 2)

    @pl.when(jnp.logical_or(z == 0, z == last))
    def _():
        pl.semaphore_wait(barrier, n_section + 1)

    signal_up = remote(
        signal.at[length - EDGE : length], ext.at[0:EDGE], halo_sem.at[0], halo_sem.at[1], to_seq(z + 1)
    )
    signal_down = remote(
        signal.at[0:EDGE], ext.at[end : end + EDGE], halo_sem.at[2], halo_sem.at[3], to_seq(z - 1)
    )

    @pl.when(z < last)
    def _():
        signal_up.start()

    @pl.when(z > 0)
    def _():
        signal_down.start()

    trunk_copies = []
    for step in range(1, n_section):
        target = lax.rem(s + step, n_section)
        copy = remote(
            trunk.at[:, pl.ds(pl.multiple_of(target * c_out, 128), c_out)],
            pooled.at[own_rows],
            trunk_sem.at[0, step - 1],
            trunk_sem.at[1, step - 1],
            to_section(target),
        )
        copy.start()
        trunk_copies.append(copy)

    signal_cross = remote(
        signal.at[pl.ds(pl.multiple_of(core * part, EDGE), part), theirs],
        other.at[pl.ds(pl.multiple_of(EDGE + core * part, EDGE), part)],
        signal_sem.at[0],
        signal_sem.at[1],
        to_dp(),
    )
    signal_cross.start()
    brought = other.at[pl.ds(pl.multiple_of(EDGE + core * part, EDGE), part)]
    signal_pass = remote(brought, brought, signal_sem.at[2], signal_sem.at[3], to_section(sibling))
    edge_low = remote(
        ext.at[0:EDGE, theirs], other.at[0:EDGE], signal_sem.at[4], signal_sem.at[5], to_dp()
    )
    edge_high = remote(
        ext.at[end : end + EDGE, theirs],
        other.at[end : end + EDGE],
        signal_sem.at[6],
        signal_sem.at[7],
        to_dp(),
    )

    load_signal.wait()

    @pl.when(z < last)
    def _():
        signal_up.wait_send()
        signal_down.wait_recv()

    @pl.when(z > 0)
    def _():
        signal_down.wait_send()
        signal_up.wait_recv()

    edge_low.start()
    edge_high.start()
    load_flat.wait()

    for tap in range(taps):
        prod[...] = lax.dot_general(
            ext[...],
            flat[tap * c_out : (tap + 1) * c_out],
            (((1,), (1,)), ((), ())),
            preferred_element_type=f32,
        )
        moved = prod[EDGE - width + tap : EDGE - width + tap + length]
        if tap == 0:
            linear[...] = moved
        else:
            linear[...] += moved

    load_trunk.wait()
    for copy in trunk_copies:
        copy.wait()

    doubled = jnp.where(
        lax.broadcasted_iota(jnp.int32, (length, length // 2), 0) // 2
        == lax.broadcasted_iota(jnp.int32, (length, length // 2), 1),
        0.5,
        0.0,
    ).astype(bf16)
    grad_f[EDGE:end] = lax.dot_general(
        doubled, pooled[...], (((1,), (0,)), ((), ())), preferred_element_type=f32
    )
    values = linear[...]
    normal_cdf = 0.5 * (1.0 + lax.erf(values * 0.7071067811865476))
    density = jnp.exp(-0.5 * values * values) * 0.3989422804014327
    grad_b[...] = (grad_f[EDGE:end] * (normal_cdf + values * density)).astype(bf16)

    grad_up = remote(
        grad_b.at[length - EDGE : length], grad_halo.at[0], grad_sem.at[0], grad_sem.at[1], to_seq(z + 1)
    )
    grad_down = remote(
        grad_b.at[0:EDGE], grad_halo.at[1], grad_sem.at[2], grad_sem.at[3], to_seq(z - 1)
    )

    @pl.when(z < last)
    def _():
        grad_up.start()

    @pl.when(z > 0)
    def _():
        grad_down.start()

    grad_f[EDGE:end] = grad_b[...].astype(f32)
    grad_t[0] = grad_f[EDGE:end].T.astype(bf16)
    grad_cross = remote(grad_t.at[0], grad_t.at[1], grad_sem.at[4], grad_sem.at[5], to_dp())
    grad_cross.start()

    signal_cross.wait_recv()
    signal_pass.start()

    @pl.when(z < last)
    def _():
        grad_up.wait_send()
        grad_down.wait_recv()

    @pl.when(z > 0)
    def _():
        grad_down.wait_send()
        grad_up.wait_recv()

    grad_f[0:EDGE] = grad_halo[0].astype(f32)
    grad_f[end : end + EDGE] = grad_halo[1].astype(f32)
    for tap in range(taps):
        begin = EDGE + width - tap
        stacked[:, tap * c_out : (tap + 1) * c_out] = grad_f[begin : begin + length].astype(bf16)
    for column in range(0, c_in, 256):
        piece = lax.dot_general(
            stacked[...],
            flat[:, column : column + 256],
            (((1,), (0,)), ((), ())),
            preferred_element_type=f32,
        )
        input_part[column : column + 256] = piece.T.astype(bf16)
    input_copies = []
    for step in range(1, n_section):
        target = lax.rem(s + step, n_section)
        copy = remote(
            input_part.at[pl.ds(pl.multiple_of(target * block, EDGE), block)],
            input_recv.at[step - 1],
            input_sem.at[0, step - 1],
            input_sem.at[1, step - 1],
            to_section(target),
        )
        copy.start()
        input_copies.append(copy)

    shift[...] = ext[:, mine].astype(f32)
    for tap in range(taps):
        begin = EDGE - width + tap
        windows[0, tap] = shift[begin : begin + length].astype(bf16)
    signal_cross.wait_send()
    signal_pass.wait()
    edge_low.wait()
    edge_high.wait()
    shift[...] = other[...].astype(f32)
    for tap in range(taps):
        begin = EDGE - width + tap
        windows[1, tap] = shift[begin : begin + length].astype(bf16)
    grad_cross.wait()

    def up(tap, owner):
        return remote(
            ring_send.at[tap, owner],
            ring_up.at[tap, owner],
            ring_send_sem.at[tap, owner],
            ring_up_sem.at[tap, owner],
            to_seq(z + 1),
        )

    def down(tap, owner):
        return remote(
            ring_send.at[tap, owner],
            ring_down.at[tap, owner],
            ring_send_sem.at[tap, owner],
            ring_down_sem.at[tap, owner],
            to_seq(z - 1),
        )

    def own(tap, owner):
        return weight_f[tap, owner * share : (owner + 1) * share]

    for tap in range(taps):
        weight_f[tap] = jnp.dot(
            grad_t[0], windows[0, tap], preferred_element_type=f32
        ) + jnp.dot(grad_t[1], windows[1, tap], preferred_element_type=f32)

        @pl.when(z == 0)
        def _():
            for owner in range(last, 0, -1):
                ring_send[tap, owner] = own(tap, owner).astype(bf16)
                up(tap, owner).start()

        @pl.when(z == last)
        def _():
            for owner in range(0, last):
                ring_send[tap, owner] = own(tap, owner).astype(bf16)
                down(tap, owner).start()

    def finish(tap, total):
        weight_out[tap, :, mine] = total
        last_send[tap] = total.astype(bf16)

    def cross(tap):
        return remote(
            last_send.at[tap], last_recv.at[tap], last_sem.at[0, tap], last_sem.at[1, tap], to_dp()
        )

    def relay_up(tap, owner):
        up(tap, owner).wait_recv()
        ring_send[tap, owner] = (own(tap, owner) + ring_up[tap, owner].astype(f32)).astype(bf16)
        up(tap, owner).start()

    def relay_down(tap, owner):
        down(tap, owner).wait_recv()
        ring_send[tap, owner] = (own(tap, owner) + ring_down[tap, owner].astype(f32)).astype(bf16)
        down(tap, owner).start()

    for tap in range(taps):
        for place in range(n_seq):

            @pl.when(z == place)
            def _():
                if 0 < place < last:
                    ups = [(relay_up, owner) for owner in range(last, place, -1)]
                    downs = [(relay_down, owner) for owner in range(0, place)]
                    order = ups + downs if place < n_seq // 2 else downs + ups
                    for relay, owner in order:
                        relay(tap, owner)
                total = own(tap, place)
                if place > 0:
                    up(tap, place).wait_recv()
                    total = total + ring_up[tap, place].astype(f32)
                if place < last:
                    down(tap, place).wait_recv()
                    total = total + ring_down[tap, place].astype(f32)
                finish(tap, total)

        cross(tap).start()

        if tap == 0:
            for copy in input_copies:
                copy.wait()
            summed = input_part[pl.ds(pl.multiple_of(s * block, EDGE), block)].astype(f32)
            for step in range(1, n_section):
                summed = summed + input_recv[step - 1].astype(f32)
            input_out[...] = summed.astype(bf16)

    for tap in range(taps):
        cross(tap).wait()
        weight_out[tap, :, theirs] = last_recv[tap].astype(f32)
        for place in range(n_seq):

            @pl.when(z == place)
            def _():
                for owner in range(n_seq):
                    if owner > place:
                        up(tap, owner).wait_send()
                    elif owner < place:
                        down(tap, owner).wait_send()


def fused_shards(n_seq, n_section, signal, kernel, trunk_grad):
    f32, bf16 = jnp.float32, jnp.bfloat16
    _, length, c_in = signal.shape
    c_out, taps, _ = kernel.shape
    share, block, half = c_out // n_seq, c_in // n_section, c_in // 2
    padded = length + 2 * EDGE
    flat = jnp.transpose(kernel, (1, 0, 2)).reshape(taps * c_out, c_in)
    vmem = pl.BlockSpec(memory_space=pltpu.VMEM)
    hbm = pl.BlockSpec(memory_space=pl.ANY)
    dma = pltpu.SemaphoreType.DMA
    weight, rows = pl.pallas_call(
        functools.partial(fused_kernel, n_seq, n_section),
        out_shape=(
            jax.ShapeDtypeStruct((taps, share, c_in), f32),
            jax.ShapeDtypeStruct((block, length), bf16),
        ),
        in_specs=[hbm, hbm, hbm],
        out_specs=(vmem, vmem),
        scratch_shapes=[
            pltpu.VMEM((padded, c_in), bf16),
            pltpu.VMEM((taps * c_out, c_in), bf16),
            pltpu.VMEM((length // 2, c_out), bf16),
            pltpu.VMEM((padded, c_out), f32),
            pltpu.VMEM((length, c_out), f32),
            pltpu.VMEM((length, c_out), bf16),
            pltpu.VMEM((padded, c_out), f32),
            pltpu.VMEM((2, EDGE, c_out), bf16),
            pltpu.VMEM((length, taps * c_out), bf16),
            pltpu.VMEM((2, c_out, length), bf16),
            pltpu.VMEM((padded, half), bf16),
            pltpu.VMEM((padded, half), f32),
            pltpu.VMEM((2, taps, length, half), bf16),
            pltpu.VMEM((c_in, length), bf16),
            pltpu.VMEM((n_section - 1, block, length), bf16),
            pltpu.VMEM((taps, c_out, half), f32),
            pltpu.VMEM((taps, n_seq, share, half), bf16),
            pltpu.VMEM((taps, n_seq, share, half), bf16),
            pltpu.VMEM((taps, n_seq, share, half), bf16),
            pltpu.VMEM((taps, share, half), bf16),
            pltpu.VMEM((taps, share, half), bf16),
            dma((3,)),
            dma((4,)),
            dma((2, n_section - 1)),
            dma((8,)),
            dma((6,)),
            dma((2, n_section - 1)),
            dma((taps, n_seq)),
            dma((taps, n_seq)),
            dma((taps, n_seq)),
            dma((2, taps)),
        ],
        compiler_params=pltpu.CompilerParams(
            collective_id=0, has_side_effects=True, vmem_limit_bytes=60 * 1024 * 1024
        ),
        cost_estimate=pl.CostEstimate(
            flops=6 * length * c_in * c_out * taps,
            bytes_accessed=2 * (length * c_in + 3 * c_out * taps * c_in),
            transcendentals=2 * length * c_out,
        ),
    )(signal[0], flat, trunk_grad[0])
    return jnp.transpose(weight, (1, 0, 2)), rows[None]


def fits(mesh):
    return (mesh.shape["dp"], mesh.shape["seq"], mesh.shape["section"]) == (2, 4, 4)


def solution(mesh):
    body = shards
    if fits(mesh):
        body = functools.partial(fused_shards, mesh.shape["seq"], mesh.shape["section"])
    return jax.shard_map(
        body,
        mesh=mesh,
        in_specs=(
            P("dp", "seq", None),
            P("section", None, None),
            P("dp", ("seq", "section"), None),
        ),
        out_specs=(P(("section", "seq"), None, None), P("dp", "section", "seq")),
        check_vma=False,
    )
```

```python
import functools

import jax
import jax.numpy as jnp
from jax import lax
from jax.experimental import pallas as pl
from jax.experimental.pallas import tpu as pltpu
from jax.sharding import PartitionSpec as P


def edges(block, axis, width):
    count = lax.axis_size(axis)
    forward = [(i, i + 1) for i in range(count - 1)]
    backward = [(target, source) for source, target in forward]
    low = lax.ppermute(block[-width:], axis, forward)
    high = lax.ppermute(block[:width], axis, backward)
    return jnp.concatenate([low, block, high], axis=0)


def gelu_slope(values):
    normal_cdf = 0.5 * (1.0 + jax.scipy.special.erf(values * 0.7071067811865476))
    density = jnp.exp(-0.5 * values * values) * 0.3989422804014327
    return normal_cdf + values * density


def shards(signal, kernel, trunk_grad):
    n_dp = lax.axis_size("dp")
    n_section = lax.axis_size("section")
    me = lax.axis_index("dp")
    local = signal[0]
    length, c_in = local.shape
    c_out, taps_count, _ = kernel.shape
    width = taps_count // 2
    share = c_in // n_dp
    flat = jnp.transpose(kernel, (1, 0, 2)).reshape(taps_count * c_out, c_in)

    rows = trunk_grad.shape[1]
    trunk = jnp.transpose(trunk_grad[0].reshape(rows, n_section, c_out), (1, 0, 2))
    pooled = lax.all_to_all(trunk, "section", split_axis=0, concat_axis=0).reshape(
        n_section * rows, c_out
    )
    padded = edges(local, "seq", width)

    rings = [[(i, (i + step) % n_dp) for i in range(n_dp)] for step in range(n_dp)]

    def columns(owner):
        return lax.dynamic_slice_in_dim(padded, owner * share, share, axis=1)

    windows = [columns(me)]
    for step in range(1, n_dp):
        windows.append(lax.ppermute(columns((me + step) % n_dp), "dp", rings[step]))

    product = lax.dot_general(
        padded, flat, (((1,), (1,)), ((), ())), preferred_element_type=jnp.float32
    )
    linear = product[0:length, 0:c_out]
    for tap in range(1, taps_count):
        linear = linear + product[tap : tap + length, tap * c_out : (tap + 1) * c_out]
    grad_hidden = 0.5 * jnp.repeat(pooled.astype(jnp.float32), 2, axis=0)
    grad_pre = (grad_hidden * gelu_slope(linear)).astype(jnp.bfloat16)

    grads = [grad_pre]
    for step in range(1, n_dp):
        grads.append(lax.ppermute(grad_pre, "dp", rings[step]))
    grad_ext = edges(grad_pre, "seq", width)

    all_grads = jnp.concatenate(grads, axis=0)
    taps = []
    for tap in range(taps_count):
        window = jnp.concatenate([w[tap : tap + length] for w in windows], axis=0)
        taps.append(
            lax.dot_general(
                all_grads, window, (((0,), (0,)), ((), ())), preferred_element_type=jnp.float32
            ).astype(jnp.bfloat16)
        )
    partial = jnp.stack(taps, axis=1)
    weight_rows = lax.psum_scatter(partial, "seq", scatter_dimension=0, tiled=True)

    stacked = jnp.concatenate(
        [grad_ext[2 * width - tap : 2 * width - tap + length] for tap in range(taps_count)], axis=1
    )
    summed = lax.dot_general(
        flat, stacked, (((0,), (1,)), ((), ())), preferred_element_type=jnp.float32
    ).astype(jnp.bfloat16)
    input_rows = lax.psum_scatter(summed, "section", scatter_dimension=0, tiled=True)

    weight_grad = jnp.zeros(weight_rows.shape[:2] + (c_in,), jnp.float32)
    weight_grad = lax.dynamic_update_slice_in_dim(
        weight_grad, weight_rows.astype(jnp.float32), me * share, axis=2
    )
    for step in range(1, n_dp):
        other = lax.ppermute(weight_rows, "dp", rings[step])
        weight_grad = lax.dynamic_update_slice_in_dim(
            weight_grad, other.astype(jnp.float32), ((me - step) % n_dp) * share, axis=2
        )
    return (weight_grad, input_rows[None])


MESH = pl.DeviceIdType.MESH
EDGE = 16


def fused_kernel(
    n_seq,
    n_section,
    signal,
    flat_hbm,
    trunk,
    weight_out,
    input_out,
    ext,
    flat,
    pooled,
    prod,
    linear,
    grad_b,
    grad_f,
    grad_halo,
    stacked,
    grad_t,
    other,
    shift,
    windows,
    input_part,
    input_recv,
    weight_f,
    ring_send,
    ring_up,
    ring_down,
    load_sem,
    halo_sem,
    trunk_sem,
    signal_sem,
    grad_sem,
    input_sem,
    ring_send_sem,
    ring_up_sem,
    ring_down_sem,
    last_sem,
):
    f32, bf16 = jnp.float32, jnp.bfloat16
    d, z, s = lax.axis_index("dp"), lax.axis_index("seq"), lax.axis_index("section")
    length, c_in = signal.shape
    c_out = pooled.shape[1]
    rows = trunk.shape[0]
    taps = flat.shape[0] // c_out
    half = c_in // 2
    part = length // 2
    width = taps // 2
    share = c_out // n_seq
    band = c_out // 2
    block = c_in // n_section
    end = EDGE + length
    core = lax.rem(s, 2)
    sibling = s + 1 - 2 * core
    last = n_seq - 1

    def to_dp():
        return {"dp": 1 - d}

    def to_seq(target):
        return {"seq": target}

    def to_section(target):
        return {"section": target}

    def remote(src, dst, send, recv, target):
        return pltpu.make_async_remote_copy(
            src_ref=src,
            dst_ref=dst,
            send_sem=send,
            recv_sem=recv,
            device_id=target,
            device_id_type=MESH,
        )

    mine = pl.ds(pl.multiple_of(d * half, 128), half)
    theirs = pl.ds(pl.multiple_of((1 - d) * half, 128), half)
    own_rows = pl.ds(pl.multiple_of(s * rows, EDGE), rows)

    load_signal = pltpu.make_async_copy(signal, ext.at[EDGE:end], load_sem.at[0])
    load_flat = pltpu.make_async_copy(flat_hbm, flat, load_sem.at[1])
    load_trunk = pltpu.make_async_copy(
        trunk.at[:, pl.ds(pl.multiple_of(s * c_out, 128), c_out)], pooled.at[own_rows], load_sem.at[2]
    )
    load_signal.start()
    load_flat.start()
    load_trunk.start()

    @pl.when(z == 0)
    def _():
        ext[0:EDGE] = jnp.zeros((EDGE, c_in), bf16)
        grad_halo[0] = jnp.zeros((EDGE, c_out), bf16)

    @pl.when(z == last)
    def _():
        ext[end : end + EDGE] = jnp.zeros((EDGE, c_in), bf16)
        grad_halo[1] = jnp.zeros((EDGE, c_out), bf16)

    barrier = pltpu.get_barrier_semaphore()
    pl.semaphore_signal(barrier, inc=1, device_id=to_dp(), device_id_type=MESH)
    for step in range(1, n_section):
        pl.semaphore_signal(
            barrier, inc=1, device_id=to_section(lax.rem(s + step, n_section)), device_id_type=MESH
        )

    @pl.when(z > 0)
    def _():
        pl.semaphore_signal(barrier, inc=1, device_id=to_seq(z - 1), device_id_type=MESH)

    @pl.when(z < last)
    def _():
        pl.semaphore_signal(barrier, inc=1, device_id=to_seq(z + 1), device_id_type=MESH)

    @pl.when(jnp.logical_and(z > 0, z < last))
    def _():
        pl.semaphore_wait(barrier, n_section + 2)

    @pl.when(jnp.logical_or(z == 0, z == last))
    def _():
        pl.semaphore_wait(barrier, n_section + 1)

    signal_up = remote(
        signal.at[length - EDGE : length], ext.at[0:EDGE], halo_sem.at[0], halo_sem.at[1], to_seq(z + 1)
    )
    signal_down = remote(
        signal.at[0:EDGE], ext.at[end : end + EDGE], halo_sem.at[2], halo_sem.at[3], to_seq(z - 1)
    )

    @pl.when(z < last)
    def _():
        signal_up.start()

    @pl.when(z > 0)
    def _():
        signal_down.start()

    trunk_copies = []
    for step in range(1, n_section):
        target = lax.rem(s + step, n_section)
        copy = remote(
            trunk.at[:, pl.ds(pl.multiple_of(target * c_out, 128), c_out)],
            pooled.at[own_rows],
            trunk_sem.at[0, step - 1],
            trunk_sem.at[1, step - 1],
            to_section(target),
        )
        copy.start()
        trunk_copies.append(copy)

    signal_cross = remote(
        signal.at[pl.ds(pl.multiple_of(core * part, EDGE), part), theirs],
        other.at[pl.ds(pl.multiple_of(EDGE + core * part, EDGE), part)],
        signal_sem.at[0],
        signal_sem.at[1],
        to_dp(),
    )
    signal_cross.start()
    brought = other.at[pl.ds(pl.multiple_of(EDGE + core * part, EDGE), part)]
    signal_pass = remote(brought, brought, signal_sem.at[2], signal_sem.at[3], to_section(sibling))
    edge_low = remote(
        ext.at[0:EDGE, theirs], other.at[0:EDGE], signal_sem.at[4], signal_sem.at[5], to_dp()
    )
    edge_high = remote(
        ext.at[end : end + EDGE, theirs],
        other.at[end : end + EDGE],
        signal_sem.at[6],
        signal_sem.at[7],
        to_dp(),
    )

    load_signal.wait()

    @pl.when(z < last)
    def _():
        signal_up.wait_send()
        signal_down.wait_recv()

    @pl.when(z > 0)
    def _():
        signal_down.wait_send()
        signal_up.wait_recv()

    edge_low.start()
    edge_high.start()
    load_flat.wait()

    for tap in range(taps):
        prod[...] = lax.dot_general(
            ext[...],
            flat[tap * c_out : (tap + 1) * c_out],
            (((1,), (1,)), ((), ())),
            preferred_element_type=f32,
        )
        moved = prod[EDGE - width + tap : EDGE - width + tap + length]
        if tap == 0:
            linear[...] = moved
        else:
            linear[...] += moved

    load_trunk.wait()
    for copy in trunk_copies:
        copy.wait()

    doubled = jnp.where(
        lax.broadcasted_iota(jnp.int32, (length, length // 2), 0) // 2
        == lax.broadcasted_iota(jnp.int32, (length, length // 2), 1),
        0.5,
        0.0,
    ).astype(bf16)
    grad_f[EDGE:end] = lax.dot_general(
        doubled, pooled[...], (((1,), (0,)), ((), ())), preferred_element_type=f32
    )
    values = linear[...]
    normal_cdf = 0.5 * (1.0 + lax.erf(values * 0.7071067811865476))
    density = jnp.exp(-0.5 * values * values) * 0.3989422804014327
    grad_b[...] = (grad_f[EDGE:end] * (normal_cdf + values * density)).astype(bf16)

    grad_up = remote(
        grad_b.at[length - EDGE : length], grad_halo.at[0], grad_sem.at[0], grad_sem.at[1], to_seq(z + 1)
    )
    grad_down = remote(
        grad_b.at[0:EDGE], grad_halo.at[1], grad_sem.at[2], grad_sem.at[3], to_seq(z - 1)
    )

    @pl.when(z < last)
    def _():
        grad_up.start()

    @pl.when(z > 0)
    def _():
        grad_down.start()

    grad_f[EDGE:end] = grad_b[...].astype(f32)
    grad_t[0] = grad_f[EDGE:end].T.astype(bf16)
    first = jnp.where(z < n_seq // 2, 1, 0)
    bands = [pl.ds(pl.multiple_of(at * band, EDGE), band) for at in (first, 1 - first)]
    grad_crosses = []
    for at in range(2):
        copy = remote(
            grad_t.at[0, bands[at]],
            grad_t.at[1, bands[at]],
            grad_sem.at[4 + 2 * at],
            grad_sem.at[5 + 2 * at],
            to_dp(),
        )
        copy.start()
        grad_crosses.append(copy)

    signal_cross.wait_recv()
    signal_pass.start()

    shift[0] = ext[:, mine].astype(f32)
    signal_cross.wait_send()
    signal_pass.wait()
    edge_low.wait()
    edge_high.wait()
    shift[1] = other[...].astype(f32)

    def up(tap, owner):
        return remote(
            ring_send.at[tap, owner],
            ring_up.at[tap, owner],
            ring_send_sem.at[tap, owner],
            ring_up_sem.at[tap, owner],
            to_seq(z + 1),
        )

    def down(tap, owner):
        return remote(
            ring_send.at[tap, owner],
            ring_down.at[tap, owner],
            ring_send_sem.at[tap, owner],
            ring_down_sem.at[tap, owner],
            to_seq(z - 1),
        )

    def own(tap, owner):
        return weight_f[tap, owner * share : (owner + 1) * share]

    def finish(tap, total):
        weight_out[tap, :, mine] = total.astype(bf16)

    def cross(tap):
        return remote(
            weight_out.at[tap, :, mine], weight_out.at[tap, :, mine], last_sem.at[0, tap], last_sem.at[1, tap], to_dp()
        )

    def relay_up(tap, owner):
        up(tap, owner).wait_recv()
        ring_send[tap, owner] = (own(tap, owner) + ring_up[tap, owner].astype(f32)).astype(bf16)
        up(tap, owner).start()

    def relay_down(tap, owner):
        down(tap, owner).wait_recv()
        ring_send[tap, owner] = (own(tap, owner) + ring_down[tap, owner].astype(f32)).astype(bf16)
        down(tap, owner).start()

    def multiply(tap, at):
        weight_f[tap, bands[at]] = jnp.dot(
            grad_t[0, bands[at]], windows[0, tap], preferred_element_type=f32
        ) + jnp.dot(grad_t[1, bands[at]], windows[1, tap], preferred_element_type=f32)

    def send_up(tap, owners):
        for owner in owners:
            ring_send[tap, owner] = own(tap, owner).astype(bf16)
            up(tap, owner).start()

    def send_down(tap, owners):
        for owner in owners:
            ring_send[tap, owner] = own(tap, owner).astype(bf16)
            down(tap, owner).start()

    def relay(tap, place, band_at):
        low_band = range(0, n_seq // 2)
        owners = low_band if (place >= n_seq // 2) == (band_at == 0) else range(n_seq // 2, n_seq)
        for owner in reversed(owners):
            if owner > place:
                relay_up(tap, owner)
        for owner in owners:
            if owner < place:
                relay_down(tap, owner)

    middle = n_seq // 2
    for tap in range(taps):
        begin = EDGE - width + tap
        for source in range(2):
            windows[source, tap] = shift[source, begin : begin + length].astype(bf16)
        if tap == 0:
            grad_crosses[0].wait()
        multiply(tap, 0)

        @pl.when(z == 0)
        def _():
            send_up(tap, range(last, middle - 1, -1))

        @pl.when(z == last)
        def _():
            send_down(tap, range(0, middle))

    @pl.when(z < last)
    def _():
        grad_up.wait_send()
        grad_down.wait_recv()

    @pl.when(z > 0)
    def _():
        grad_down.wait_send()
        grad_up.wait_recv()

    grad_f[0:EDGE] = grad_halo[0].astype(f32)
    grad_f[end : end + EDGE] = grad_halo[1].astype(f32)
    for tap in range(taps):
        begin = EDGE + width - tap
        stacked[:, tap * c_out : (tap + 1) * c_out] = grad_f[begin : begin + length].astype(bf16)

    def input_columns(column):
        piece = lax.dot_general(
            stacked[...],
            flat[:, column : column + 256],
            (((1,), (0,)), ((), ())),
            preferred_element_type=f32,
        )
        input_part[column : column + 256] = piece.T.astype(bf16)

    input_copies = []
    pending = list(range(0, c_in, 256))
    grad_crosses[1].wait()
    for tap in range(taps):
        multiply(tap, 1)

        @pl.when(z == 0)
        def _():
            send_up(tap, range(middle - 1, 0, -1))

        @pl.when(z == last)
        def _():
            send_down(tap, range(middle, last))

        if pending:
            for column in pending[:2]:
                input_columns(column)
            pending = pending[2:]
            if not pending:
                for step in range(1, n_section):
                    target = lax.rem(s + step, n_section)
                    copy = remote(
                        input_part.at[pl.ds(pl.multiple_of(target * block, EDGE), block)],
                        input_recv.at[step - 1],
                        input_sem.at[0, step - 1],
                        input_sem.at[1, step - 1],
                        to_section(target),
                    )
                    copy.start()
                    input_copies.append(copy)

        for place in range(1, last):

            @pl.when(z == place)
            def _():
                relay(tap, place, 0)

    for tap in range(taps):
        for place in range(n_seq):

            @pl.when(z == place)
            def _():
                if 0 < place < last:
                    relay(tap, place, 1)
                total = own(tap, place)
                if place > 0:
                    up(tap, place).wait_recv()
                    total = total + ring_up[tap, place].astype(f32)
                if place < last:
                    down(tap, place).wait_recv()
                    total = total + ring_down[tap, place].astype(f32)
                finish(tap, total)

        cross(tap).start()

    for copy in input_copies:
        copy.wait()
    summed = input_part[pl.ds(pl.multiple_of(s * block, EDGE), block)].astype(f32)
    for step in range(1, n_section):
        summed = summed + input_recv[step - 1].astype(f32)
    input_out[...] = summed.astype(bf16)

    for tap in range(taps):
        cross(tap).wait()
        for place in range(n_seq):

            @pl.when(z == place)
            def _():
                for owner in range(n_seq):
                    if owner > place:
                        up(tap, owner).wait_send()
                    elif owner < place:
                        down(tap, owner).wait_send()


def fused_shards(n_seq, n_section, signal, kernel, trunk_grad):
    f32, bf16 = jnp.float32, jnp.bfloat16
    _, length, c_in = signal.shape
    c_out, taps, _ = kernel.shape
    share, block, half = c_out // n_seq, c_in // n_section, c_in // 2
    padded = length + 2 * EDGE
    flat = jnp.transpose(kernel, (1, 0, 2)).reshape(taps * c_out, c_in)
    vmem = pl.BlockSpec(memory_space=pltpu.VMEM)
    hbm = pl.BlockSpec(memory_space=pl.ANY)
    dma = pltpu.SemaphoreType.DMA
    weight, rows = pl.pallas_call(
        functools.partial(fused_kernel, n_seq, n_section),
        out_shape=(
            jax.ShapeDtypeStruct((taps, share, c_in), bf16),
            jax.ShapeDtypeStruct((block, length), bf16),
        ),
        in_specs=[hbm, hbm, hbm],
        out_specs=(vmem, vmem),
        scratch_shapes=[
            pltpu.VMEM((padded, c_in), bf16),
            pltpu.VMEM((taps * c_out, c_in), bf16),
            pltpu.VMEM((length // 2, c_out), bf16),
            pltpu.VMEM((padded, c_out), f32),
            pltpu.VMEM((length, c_out), f32),
            pltpu.VMEM((length, c_out), bf16),
            pltpu.VMEM((padded, c_out), f32),
            pltpu.VMEM((2, EDGE, c_out), bf16),
            pltpu.VMEM((length, taps * c_out), bf16),
            pltpu.VMEM((2, c_out, length), bf16),
            pltpu.VMEM((padded, half), bf16),
            pltpu.VMEM((2, padded, half), f32),
            pltpu.VMEM((2, taps, length, half), bf16),
            pltpu.VMEM((c_in, length), bf16),
            pltpu.VMEM((n_section - 1, block, length), bf16),
            pltpu.VMEM((taps, c_out, half), f32),
            pltpu.VMEM((taps, n_seq, share, half), bf16),
            pltpu.VMEM((taps, n_seq, share, half), bf16),
            pltpu.VMEM((taps, n_seq, share, half), bf16),
            dma((3,)),
            dma((4,)),
            dma((2, n_section - 1)),
            dma((8,)),
            dma((8,)),
            dma((2, n_section - 1)),
            dma((taps, n_seq)),
            dma((taps, n_seq)),
            dma((taps, n_seq)),
            dma((2, taps)),
        ],
        compiler_params=pltpu.CompilerParams(
            collective_id=0, has_side_effects=True, vmem_limit_bytes=60 * 1024 * 1024
        ),
        cost_estimate=pl.CostEstimate(
            flops=6 * length * c_in * c_out * taps,
            bytes_accessed=2 * (length * c_in + 3 * c_out * taps * c_in),
            transcendentals=2 * length * c_out,
        ),
    )(signal[0], flat, trunk_grad[0])
    return jnp.transpose(weight.astype(f32), (1, 0, 2)), rows[None]


def fits(mesh):
    return (mesh.shape["dp"], mesh.shape["seq"], mesh.shape["section"]) == (2, 4, 4)


def solution(mesh):
    body = shards
    if fits(mesh):
        body = functools.partial(fused_shards, mesh.shape["seq"], mesh.shape["section"])
    return jax.shard_map(
        body,
        mesh=mesh,
        in_specs=(
            P("dp", "seq", None),
            P("section", None, None),
            P("dp", ("seq", "section"), None),
        ),
        out_specs=(P(("section", "seq"), None, None), P("dp", "section", "seq")),
        check_vma=False,
    )
```

```python
import functools

import jax
import jax.numpy as jnp
from jax import lax
from jax.experimental import pallas as pl
from jax.experimental.pallas import tpu as pltpu
from jax.sharding import PartitionSpec as P


def edges(block, axis, width):
    count = lax.axis_size(axis)
    forward = [(i, i + 1) for i in range(count - 1)]
    backward = [(target, source) for source, target in forward]
    low = lax.ppermute(block[-width:], axis, forward)
    high = lax.ppermute(block[:width], axis, backward)
    return jnp.concatenate([low, block, high], axis=0)


def gelu_slope(values):
    normal_cdf = 0.5 * (1.0 + jax.scipy.special.erf(values * 0.7071067811865476))
    density = jnp.exp(-0.5 * values * values) * 0.3989422804014327
    return normal_cdf + values * density


def shards(signal, kernel, trunk_grad):
    n_dp = lax.axis_size("dp")
    n_section = lax.axis_size("section")
    me = lax.axis_index("dp")
    local = signal[0]
    length, c_in = local.shape
    c_out, taps_count, _ = kernel.shape
    width = taps_count // 2
    share = c_in // n_dp
    flat = jnp.transpose(kernel, (1, 0, 2)).reshape(taps_count * c_out, c_in)

    rows = trunk_grad.shape[1]
    trunk = jnp.transpose(trunk_grad[0].reshape(rows, n_section, c_out), (1, 0, 2))
    pooled = lax.all_to_all(trunk, "section", split_axis=0, concat_axis=0).reshape(
        n_section * rows, c_out
    )
    padded = edges(local, "seq", width)

    rings = [[(i, (i + step) % n_dp) for i in range(n_dp)] for step in range(n_dp)]

    def columns(owner):
        return lax.dynamic_slice_in_dim(padded, owner * share, share, axis=1)

    windows = [columns(me)]
    for step in range(1, n_dp):
        windows.append(lax.ppermute(columns((me + step) % n_dp), "dp", rings[step]))

    product = lax.dot_general(
        padded, flat, (((1,), (1,)), ((), ())), preferred_element_type=jnp.float32
    )
    linear = product[0:length, 0:c_out]
    for tap in range(1, taps_count):
        linear = linear + product[tap : tap + length, tap * c_out : (tap + 1) * c_out]
    grad_hidden = 0.5 * jnp.repeat(pooled.astype(jnp.float32), 2, axis=0)
    grad_pre = (grad_hidden * gelu_slope(linear)).astype(jnp.bfloat16)

    grads = [grad_pre]
    for step in range(1, n_dp):
        grads.append(lax.ppermute(grad_pre, "dp", rings[step]))
    grad_ext = edges(grad_pre, "seq", width)

    all_grads = jnp.concatenate(grads, axis=0)
    taps = []
    for tap in range(taps_count):
        window = jnp.concatenate([w[tap : tap + length] for w in windows], axis=0)
        taps.append(
            lax.dot_general(
                all_grads, window, (((0,), (0,)), ((), ())), preferred_element_type=jnp.float32
            ).astype(jnp.bfloat16)
        )
    partial = jnp.stack(taps, axis=1)
    weight_rows = lax.psum_scatter(partial, "seq", scatter_dimension=0, tiled=True)

    stacked = jnp.concatenate(
        [grad_ext[2 * width - tap : 2 * width - tap + length] for tap in range(taps_count)], axis=1
    )
    summed = lax.dot_general(
        flat, stacked, (((0,), (1,)), ((), ())), preferred_element_type=jnp.float32
    ).astype(jnp.bfloat16)
    input_rows = lax.psum_scatter(summed, "section", scatter_dimension=0, tiled=True)

    weight_grad = jnp.zeros(weight_rows.shape[:2] + (c_in,), jnp.float32)
    weight_grad = lax.dynamic_update_slice_in_dim(
        weight_grad, weight_rows.astype(jnp.float32), me * share, axis=2
    )
    for step in range(1, n_dp):
        other = lax.ppermute(weight_rows, "dp", rings[step])
        weight_grad = lax.dynamic_update_slice_in_dim(
            weight_grad, other.astype(jnp.float32), ((me - step) % n_dp) * share, axis=2
        )
    return (weight_grad, input_rows[None])


MESH = pl.DeviceIdType.MESH
EDGE = 16


def fused_kernel(
    n_seq,
    n_section,
    signal,
    flat_hbm,
    trunk,
    weight_out,
    input_out,
    ext,
    flat,
    pooled,
    prod,
    linear,
    grad_b,
    grad_f,
    grad_halo,
    stacked,
    grad_t,
    other,
    shift,
    windows,
    input_part,
    input_recv,
    weight_f,
    ring_send,
    ring_up,
    ring_down,
    load_sem,
    halo_sem,
    trunk_sem,
    signal_sem,
    grad_sem,
    input_sem,
    ring_send_sem,
    ring_up_sem,
    ring_down_sem,
    last_sem,
):
    f32, bf16 = jnp.float32, jnp.bfloat16
    d, z, s = lax.axis_index("dp"), lax.axis_index("seq"), lax.axis_index("section")
    length, c_in = signal.shape
    c_out = pooled.shape[1]
    rows = trunk.shape[0]
    taps = flat.shape[0] // c_out
    half = c_in // 2
    part = length // 2
    width = taps // 2
    share = c_out // n_seq
    band = c_out // 2
    block = c_in // n_section
    end = EDGE + length
    core = lax.rem(s, 2)
    sibling = s + 1 - 2 * core
    last = n_seq - 1

    def to_dp():
        return {"dp": 1 - d}

    def to_seq(target):
        return {"seq": target}

    def to_section(target):
        return {"section": target}

    def remote(src, dst, send, recv, target):
        return pltpu.make_async_remote_copy(
            src_ref=src,
            dst_ref=dst,
            send_sem=send,
            recv_sem=recv,
            device_id=target,
            device_id_type=MESH,
        )

    mine = pl.ds(pl.multiple_of(d * half, 128), half)
    theirs = pl.ds(pl.multiple_of((1 - d) * half, 128), half)
    own_rows = pl.ds(pl.multiple_of(s * rows, EDGE), rows)

    load_signal = pltpu.make_async_copy(signal, ext.at[EDGE:end], load_sem.at[0])
    load_flat = pltpu.make_async_copy(flat_hbm, flat, load_sem.at[1])
    load_trunk = pltpu.make_async_copy(
        trunk.at[:, pl.ds(pl.multiple_of(s * c_out, 128), c_out)], pooled.at[own_rows], load_sem.at[2]
    )
    load_signal.start()
    load_flat.start()
    load_trunk.start()

    @pl.when(z == 0)
    def _():
        ext[0:EDGE] = jnp.zeros((EDGE, c_in), bf16)
        grad_halo[0] = jnp.zeros((EDGE, c_out), bf16)

    @pl.when(z == last)
    def _():
        ext[end : end + EDGE] = jnp.zeros((EDGE, c_in), bf16)
        grad_halo[1] = jnp.zeros((EDGE, c_out), bf16)

    barrier = pltpu.get_barrier_semaphore()
    pl.semaphore_signal(barrier, inc=1, device_id=to_dp(), device_id_type=MESH)
    for step in range(1, n_section):
        pl.semaphore_signal(
            barrier, inc=1, device_id=to_section(lax.rem(s + step, n_section)), device_id_type=MESH
        )

    @pl.when(z > 0)
    def _():
        pl.semaphore_signal(barrier, inc=1, device_id=to_seq(z - 1), device_id_type=MESH)

    @pl.when(z < last)
    def _():
        pl.semaphore_signal(barrier, inc=1, device_id=to_seq(z + 1), device_id_type=MESH)

    @pl.when(jnp.logical_and(z > 0, z < last))
    def _():
        pl.semaphore_wait(barrier, n_section + 2)

    @pl.when(jnp.logical_or(z == 0, z == last))
    def _():
        pl.semaphore_wait(barrier, n_section + 1)

    signal_up = remote(
        signal.at[length - EDGE : length], ext.at[0:EDGE], halo_sem.at[0], halo_sem.at[1], to_seq(z + 1)
    )
    signal_down = remote(
        signal.at[0:EDGE], ext.at[end : end + EDGE], halo_sem.at[2], halo_sem.at[3], to_seq(z - 1)
    )

    @pl.when(z < last)
    def _():
        signal_up.start()

    @pl.when(z > 0)
    def _():
        signal_down.start()

    trunk_copies = []
    for step in range(1, n_section):
        target = lax.rem(s + step, n_section)
        copy = remote(
            trunk.at[:, pl.ds(pl.multiple_of(target * c_out, 128), c_out)],
            pooled.at[own_rows],
            trunk_sem.at[0, step - 1],
            trunk_sem.at[1, step - 1],
            to_section(target),
        )
        copy.start()
        trunk_copies.append(copy)

    signal_cross = remote(
        signal.at[pl.ds(pl.multiple_of(core * part, EDGE), part), theirs],
        other.at[pl.ds(pl.multiple_of(EDGE + core * part, EDGE), part)],
        signal_sem.at[0],
        signal_sem.at[1],
        to_dp(),
    )
    signal_cross.start()
    brought = other.at[pl.ds(pl.multiple_of(EDGE + core * part, EDGE), part)]
    signal_pass = remote(brought, brought, signal_sem.at[2], signal_sem.at[3], to_section(sibling))
    edge_low = remote(
        ext.at[0:EDGE, theirs], other.at[0:EDGE], signal_sem.at[4], signal_sem.at[5], to_dp()
    )
    edge_high = remote(
        ext.at[end : end + EDGE, theirs],
        other.at[end : end + EDGE],
        signal_sem.at[6],
        signal_sem.at[7],
        to_dp(),
    )

    load_signal.wait()

    @pl.when(z < last)
    def _():
        signal_up.wait_send()
        signal_down.wait_recv()

    @pl.when(z > 0)
    def _():
        signal_down.wait_send()
        signal_up.wait_recv()

    edge_low.start()
    edge_high.start()
    load_flat.wait()

    first = jnp.where(z < n_seq // 2, 1, 0)
    halves = [first, 1 - first]
    bands = [pl.ds(pl.multiple_of(at * band, EDGE), band) for at in halves]
    grad_crosses = []
    for at in range(2):
        for tap in range(taps):
            prod[:, 0:band] = lax.dot_general(
                ext[...],
                flat[pl.ds(pl.multiple_of(tap * c_out + halves[at] * band, EDGE), band)],
                (((1,), (1,)), ((), ())),
                preferred_element_type=f32,
            )
            moved = prod[EDGE - width + tap : EDGE - width + tap + length, 0:band]
            if tap == 0:
                linear[:, 0:band] = moved
            else:
                linear[:, 0:band] += moved
        if at == 0:
            load_trunk.wait()
            for copy in trunk_copies:
                copy.wait()
            doubled = jnp.where(
                lax.broadcasted_iota(jnp.int32, (length, length // 2), 0) // 2
                == lax.broadcasted_iota(jnp.int32, (length, length // 2), 1),
                0.5,
                0.0,
            ).astype(bf16)
            grad_f[EDGE:end] = lax.dot_general(
                doubled, pooled[...], (((1,), (0,)), ((), ())), preferred_element_type=f32
            )
        hidden = jnp.where(
            halves[at] == 1, grad_f[EDGE:end, band : 2 * band], grad_f[EDGE:end, 0:band]
        )
        values = linear[:, 0:band]
        normal_cdf = 0.5 * (1.0 + lax.erf(values * 0.7071067811865476))
        density = jnp.exp(-0.5 * values * values) * 0.3989422804014327
        banded = hidden * (normal_cdf + values * density)
        grad_t[0, bands[at]] = banded.T.astype(bf16)
        copy = remote(
            grad_t.at[0, bands[at]],
            grad_t.at[1, bands[at]],
            grad_sem.at[4 + 2 * at],
            grad_sem.at[5 + 2 * at],
            to_dp(),
        )
        copy.start()
        grad_crosses.append(copy)

    grad_f[EDGE:end] = grad_t[0].astype(f32).T
    grad_b[...] = grad_f[EDGE:end].astype(bf16)

    grad_up = remote(
        grad_b.at[length - EDGE : length], grad_halo.at[0], grad_sem.at[0], grad_sem.at[1], to_seq(z + 1)
    )
    grad_down = remote(
        grad_b.at[0:EDGE], grad_halo.at[1], grad_sem.at[2], grad_sem.at[3], to_seq(z - 1)
    )

    @pl.when(z < last)
    def _():
        grad_up.start()

    @pl.when(z > 0)
    def _():
        grad_down.start()

    signal_cross.wait_recv()
    signal_pass.start()

    shift[0] = ext[:, mine].astype(f32)
    signal_cross.wait_send()
    signal_pass.wait()
    edge_low.wait()
    edge_high.wait()
    shift[1] = other[...].astype(f32)

    def up(tap, owner):
        return remote(
            ring_send.at[tap, owner],
            ring_up.at[tap, owner],
            ring_send_sem.at[tap, owner],
            ring_up_sem.at[tap, owner],
            to_seq(z + 1),
        )

    def down(tap, owner):
        return remote(
            ring_send.at[tap, owner],
            ring_down.at[tap, owner],
            ring_send_sem.at[tap, owner],
            ring_down_sem.at[tap, owner],
            to_seq(z - 1),
        )

    def own(tap, owner):
        return weight_f[tap, owner * share : (owner + 1) * share]

    def finish(tap, total):
        weight_out[tap, :, mine] = total.astype(bf16)

    def cross(tap):
        return remote(
            weight_out.at[tap, :, mine], weight_out.at[tap, :, mine], last_sem.at[0, tap], last_sem.at[1, tap], to_dp()
        )

    def relay_up(tap, owner):
        up(tap, owner).wait_recv()
        ring_send[tap, owner] = (own(tap, owner) + ring_up[tap, owner].astype(f32)).astype(bf16)
        up(tap, owner).start()

    def relay_down(tap, owner):
        down(tap, owner).wait_recv()
        ring_send[tap, owner] = (own(tap, owner) + ring_down[tap, owner].astype(f32)).astype(bf16)
        down(tap, owner).start()

    def multiply(tap, at):
        weight_f[tap, bands[at]] = jnp.dot(
            grad_t[0, bands[at]], windows[0, tap], preferred_element_type=f32
        ) + jnp.dot(grad_t[1, bands[at]], windows[1, tap], preferred_element_type=f32)

    def send_up(tap, owners):
        for owner in owners:
            ring_send[tap, owner] = own(tap, owner).astype(bf16)
            up(tap, owner).start()

    def send_down(tap, owners):
        for owner in owners:
            ring_send[tap, owner] = own(tap, owner).astype(bf16)
            down(tap, owner).start()

    def relay(tap, place, band_at):
        low_band = range(0, n_seq // 2)
        owners = low_band if (place >= n_seq // 2) == (band_at == 0) else range(n_seq // 2, n_seq)
        for owner in reversed(owners):
            if owner > place:
                relay_up(tap, owner)
        for owner in owners:
            if owner < place:
                relay_down(tap, owner)

    middle = n_seq // 2
    for tap in range(taps):
        begin = EDGE - width + tap
        for source in range(2):
            windows[source, tap] = shift[source, begin : begin + length].astype(bf16)
        if tap == 0:
            grad_crosses[0].wait()
        multiply(tap, 0)

        @pl.when(z == 0)
        def _():
            send_up(tap, range(last, middle - 1, -1))

        @pl.when(z == last)
        def _():
            send_down(tap, range(0, middle))

    @pl.when(z < last)
    def _():
        grad_up.wait_send()
        grad_down.wait_recv()

    @pl.when(z > 0)
    def _():
        grad_down.wait_send()
        grad_up.wait_recv()

    grad_f[0:EDGE] = grad_halo[0].astype(f32)
    grad_f[end : end + EDGE] = grad_halo[1].astype(f32)
    for tap in range(taps):
        begin = EDGE + width - tap
        stacked[:, tap * c_out : (tap + 1) * c_out] = grad_f[begin : begin + length].astype(bf16)

    def input_columns(column):
        piece = lax.dot_general(
            stacked[...],
            flat[:, column : column + 256],
            (((1,), (0,)), ((), ())),
            preferred_element_type=f32,
        )
        input_part[column : column + 256] = piece.T.astype(bf16)

    input_copies = []
    pending = list(range(0, c_in, 256))
    grad_crosses[1].wait()
    for tap in range(taps):
        multiply(tap, 1)

        @pl.when(z == 0)
        def _():
            send_up(tap, range(middle - 1, 0, -1))

        @pl.when(z == last)
        def _():
            send_down(tap, range(middle, last))

        if pending:
            for column in pending[:2]:
                input_columns(column)
            pending = pending[2:]
            if not pending:
                for step in range(1, n_section):
                    target = lax.rem(s + step, n_section)
                    copy = remote(
                        input_part.at[pl.ds(pl.multiple_of(target * block, EDGE), block)],
                        input_recv.at[step - 1],
                        input_sem.at[0, step - 1],
                        input_sem.at[1, step - 1],
                        to_section(target),
                    )
                    copy.start()
                    input_copies.append(copy)

        for place in range(1, last):

            @pl.when(z == place)
            def _():
                relay(tap, place, 0)

    for tap in range(taps):
        for place in range(n_seq):

            @pl.when(z == place)
            def _():
                if 0 < place < last:
                    relay(tap, place, 1)
                total = own(tap, place)
                if place > 0:
                    up(tap, place).wait_recv()
                    total = total + ring_up[tap, place].astype(f32)
                if place < last:
                    down(tap, place).wait_recv()
                    total = total + ring_down[tap, place].astype(f32)
                finish(tap, total)

        cross(tap).start()

    for copy in input_copies:
        copy.wait()
    summed = input_part[pl.ds(pl.multiple_of(s * block, EDGE), block)].astype(f32)
    for step in range(1, n_section):
        summed = summed + input_recv[step - 1].astype(f32)
    input_out[...] = summed.astype(bf16)

    for tap in range(taps):
        cross(tap).wait()
        for place in range(n_seq):

            @pl.when(z == place)
            def _():
                for owner in range(n_seq):
                    if owner > place:
                        up(tap, owner).wait_send()
                    elif owner < place:
                        down(tap, owner).wait_send()


def fused_shards(n_seq, n_section, signal, kernel, trunk_grad):
    f32, bf16 = jnp.float32, jnp.bfloat16
    _, length, c_in = signal.shape
    c_out, taps, _ = kernel.shape
    share, block, half = c_out // n_seq, c_in // n_section, c_in // 2
    padded = length + 2 * EDGE
    flat = jnp.transpose(kernel, (1, 0, 2)).reshape(taps * c_out, c_in)
    vmem = pl.BlockSpec(memory_space=pltpu.VMEM)
    hbm = pl.BlockSpec(memory_space=pl.ANY)
    dma = pltpu.SemaphoreType.DMA
    weight, rows = pl.pallas_call(
        functools.partial(fused_kernel, n_seq, n_section),
        out_shape=(
            jax.ShapeDtypeStruct((taps, share, c_in), bf16),
            jax.ShapeDtypeStruct((block, length), bf16),
        ),
        in_specs=[hbm, hbm, hbm],
        out_specs=(vmem, vmem),
        scratch_shapes=[
            pltpu.VMEM((padded, c_in), bf16),
            pltpu.VMEM((taps * c_out, c_in), bf16),
            pltpu.VMEM((length // 2, c_out), bf16),
            pltpu.VMEM((padded, c_out), f32),
            pltpu.VMEM((length, c_out), f32),
            pltpu.VMEM((length, c_out), bf16),
            pltpu.VMEM((padded, c_out), f32),
            pltpu.VMEM((2, EDGE, c_out), bf16),
            pltpu.VMEM((length, taps * c_out), bf16),
            pltpu.VMEM((2, c_out, length), bf16),
            pltpu.VMEM((padded, half), bf16),
            pltpu.VMEM((2, padded, half), f32),
            pltpu.VMEM((2, taps, length, half), bf16),
            pltpu.VMEM((c_in, length), bf16),
            pltpu.VMEM((n_section - 1, block, length), bf16),
            pltpu.VMEM((taps, c_out, half), f32),
            pltpu.VMEM((taps, n_seq, share, half), bf16),
            pltpu.VMEM((taps, n_seq, share, half), bf16),
            pltpu.VMEM((taps, n_seq, share, half), bf16),
            dma((3,)),
            dma((4,)),
            dma((2, n_section - 1)),
            dma((8,)),
            dma((8,)),
            dma((2, n_section - 1)),
            dma((taps, n_seq)),
            dma((taps, n_seq)),
            dma((taps, n_seq)),
            dma((2, taps)),
        ],
        compiler_params=pltpu.CompilerParams(
            collective_id=0, has_side_effects=True, vmem_limit_bytes=60 * 1024 * 1024
        ),
        cost_estimate=pl.CostEstimate(
            flops=6 * length * c_in * c_out * taps,
            bytes_accessed=2 * (length * c_in + 3 * c_out * taps * c_in),
            transcendentals=2 * length * c_out,
        ),
    )(signal[0], flat, trunk_grad[0])
    return jnp.transpose(weight.astype(f32), (1, 0, 2)), rows[None]


def fits(mesh):
    return (mesh.shape["dp"], mesh.shape["seq"], mesh.shape["section"]) == (2, 4, 4)


def solution(mesh):
    body = shards
    if fits(mesh):
        body = functools.partial(fused_shards, mesh.shape["seq"], mesh.shape["section"])
    return jax.shard_map(
        body,
        mesh=mesh,
        in_specs=(
            P("dp", "seq", None),
            P("section", None, None),
            P("dp", ("seq", "section"), None),
        ),
        out_specs=(P(("section", "seq"), None, None), P("dp", "section", "seq")),
        check_vma=False,
    )
```
